32 devices in a mesh: dp: 4 (over y, core), section: 2 (over x), ctx: 4 (over z).
Axes of the slice: x: 2, y: 2, z: 4, core: 2. Of those that a mesh axis runs over, the one named last changes fastest.
Arguments:
- queries: bfloat16 [2, 4, 512, 4096], P('section', 'dp', 'ctx'), may hold values from -30 to 30
- keys_values: bfloat16 [2, 4, 512, 1024], P('section', 'dp', 'ctx'), may hold values from -30 to 30
- random_blocks: int32 [4, 4, 4, 4], P('dp'), may hold values from 0 to 3, as said below
- global_blocks: int32 [4, 2], P('dp'), may hold values from 0 to 3
- doc_lengths: int32 [4, 4], P('dp'), may hold values from 1 to 256, 512 in all within a row
- cotangent: bfloat16 [2, 4, 512, 4096], P('section', 'dp', 'ctx'), may hold values from -1.5 to 1.5
Outputs:
- stream: bfloat16 [2, 4, 512, 4096], P('section', 'dp', 'ctx')
- gain_grad: float32 [2, 4096], P('section')
The draws below stay inside these ranges and needn't reach their ends.
Inputs may be any that keep to these rules, and one draw needn't show every extreme that they name: `random_blocks`: for each query block, its 4 x 4 entries over all key heads name every block of the sequence exactly 4 times.
All inputs are finite; a program needn't handle non-finite values.
Results may differ from the reference program's by a relative error of at most 0.0062.
Values may be sent and summed in bfloat16 or wider, within the bound.
No kernel may reach another device: no remote copies, remote signals or barrier semaphores. Data moves between devices by JAX's collectives and lax.ppermute only.
A program may use at most 64 MiB of HBM per device.

```python
import math
import jax
import jax.numpy as jnp
import numpy as np
from jax import lax

HEADS = 32
KVH = 4
HD = 128
BLOCK = 128
RAND = 4
GLOBALS = 2
DOCS = 4
GROUP = 8
NBLK = 4
LEN = 512
SEQS = 4
SECTIONS = 2
DOC_MOST = 256


def draw_pair(key):
    base_key = jax.random.fold_in(key, 11)
    key_query, key_keys, key_values = jax.random.split(base_key, 3)
    query_shape = (SECTIONS, SEQS, LEN, KVH, GROUP, HD)
    head_shape = (SECTIONS, SEQS, LEN, KVH, HD)
    query_vals = jax.random.normal(key_query, query_shape, jnp.float32)
    key_vals = jax.random.normal(key_keys, head_shape, jnp.float32)
    value_vals = 2.0 * jax.random.normal(key_values, head_shape, jnp.float32)
    query_flat = query_vals.reshape(SECTIONS, SEQS, LEN, KVH * GROUP * HD)
    pair_flat = jnp.concatenate([key_vals.reshape(SECTIONS, SEQS, LEN, KVH * HD), value_vals.reshape(SECTIONS, SEQS, LEN, KVH * HD)], axis=-1)
    return (query_flat, pair_flat)


def draw_queries(key, part):
    return draw_pair(key)[0].astype(jnp.bfloat16)


def draw_keys_values(key, part):
    return draw_pair(key)[1].astype(jnp.bfloat16)


def draw_random_blocks(key, part):
    item_count = KVH * RAND
    key_list = jax.random.split(jax.random.fold_in(key, 23), SEQS * NBLK)
    orders = jax.vmap(lambda one_key: jax.random.permutation(one_key, item_count))(key_list)
    return (orders % NBLK).reshape(SEQS, NBLK, KVH, RAND).astype(jnp.int32)


def touch_ends(array, rng, low, high):
    place = [jax.random.randint(jax.random.fold_in(rng, axis), (), 0, length) for axis, length in enumerate(array.shape)]
    longest = array.shape.index(max(array.shape))
    beside = place[:longest] + [(place[longest] + 1) % array.shape[longest]] + place[longest + 1:]
    return array.at[tuple(place)].set(low).at[tuple(beside)].set(high)


def levels(own_key, extent, cuts, least, top_value):
    level, own = 1.0, jax.random.fold_in(own_key, 6)
    for dim, blocks in cuts:
        steps = jnp.exp(jax.random.uniform(jax.random.fold_in(own, dim), (blocks,), jnp.float32, least / len(cuts), top_value / len(cuts)))
        level = level * jnp.repeat(steps, extent[dim] // blocks).reshape([-1 if axis == dim else 1 for axis in range(len(extent))])
    return level


def length_profile(count, total, most, skew):
    loads = [(1 << 20) // math.isqrt(rank ** skew) + 1 for rank in range(2, count + 1)]
    surplus, given = total - most - (count - 1), [1] * (count - 1)
    while surplus > 0:
        movable = [i for i in range(count - 1) if given[i] < most]
        mass, remaining = sum([loads[i] for i in movable]), surplus
        for i in movable:
            addition = min(most - given[i], max(1, remaining * loads[i] // mass), surplus)
            given[i] = given[i] + addition
            surplus = surplus - addition
    return np.array([most] + given)


def ragged(own_key, number_of, total, limit, slope):
    if number_of == 2:
        one = jax.random.randint(own_key, (), max(1, total - limit), min(limit, total - 1) + 1)
        return jnp.stack([one, total - one])
    lengths = jnp.asarray(length_profile(number_of, total, limit, slope), jnp.int32)
    twos = (number_of - 1) // 2
    donor, taker = lengths[1:1 + 2 * twos:2], lengths[2:2 + 2 * twos:2]
    slack = jnp.minimum(donor - 1, limit - taker)
    shifted = jax.random.randint(jax.random.fold_in(own_key, 1), (twos,), 0, 1 << 20) % (slack + 1)
    lengths = lengths.at[1:1 + 2 * twos:2].set(donor - shifted).at[2:2 + 2 * twos:2].set(taker + shifted)
    return lengths[jax.random.permutation(jax.random.fold_in(own_key, 2), number_of)]


def noise(stream_key, shape, width, reach, shards=(), kind=jnp.bfloat16):
    array = width * jax.random.normal(stream_key, shape, jnp.float32)
    if shards:
        array = array * levels(stream_key, shape, shards, -0.22, 0.18)
    return jnp.clip(array, -reach, reach).astype(kind)


def setup_inputs(seed: int = 0) -> dict:
    arg_keys = jax.random.split(jax.random.key(seed), 7)
    queries = draw_queries(jax.random.fold_in(arg_keys[6], 71), 0)
    keys_values = draw_keys_values(jax.random.fold_in(arg_keys[6], 71), 0)
    random_blocks = draw_random_blocks(jax.random.fold_in(arg_keys[6], 71), 0)
    global_blocks = touch_ends(jax.random.randint(arg_keys[3], (SEQS, GLOBALS), 0, NBLK), jax.random.fold_in(arg_keys[3], 1), 0, NBLK - 1).astype(jnp.int32)
    doc_lengths = jax.vmap(lambda own: ragged(own, DOCS, LEN, DOC_MOST, 2))(jax.random.split(arg_keys[4], SEQS)).reshape((SEQS, DOCS)).astype(jnp.int32)
    cotangent = noise(arg_keys[5], (SECTIONS, SEQS, LEN, HEADS * HD), 0.25, 1.5, ((0, 2), (1, 4), (2, 4)))
    return {"queries": queries, "keys_values": keys_values, "random_blocks": random_blocks, "global_blocks": global_blocks, "doc_lengths": doc_lengths, "cotangent": cotangent}


def doc_index(doc_ends, positions):
    return lax.optimization_barrier(jnp.sum((doc_ends <= positions[..., None]).astype(jnp.int32), axis=-1))

def attend_block(query_rows, key_rows, value_rows, allowed):
    scores = jnp.einsum('qhgd,hkd->hgqk', query_rows, key_rows) / math.sqrt(HD)
    scores = jnp.where(allowed[:, None], scores, -1e+30)
    row_max = lax.optimization_barrier(jnp.max(scores, axis=-1, keepdims=True))
    weights = jnp.where(allowed[:, None], jnp.exp(scores - row_max), 0.0)
    weight_sum = lax.optimization_barrier(jnp.sum(weights, axis=-1))
    rounded = lax.optimization_barrier(weights.astype(jnp.bfloat16)).astype(jnp.float32)
    product = jnp.einsum('hgqk,hkd->qhgd', rounded, value_rows)
    return product / jnp.transpose(weight_sum, (2, 0, 1))[..., None]

def section_attention(query_seq, kv_seq, block_lists, global_ids, doc_ends):
    padded = jnp.pad(kv_seq, ((BLOCK, BLOCK), (0, 0)))
    blocked = kv_seq.reshape(NBLK, BLOCK, 2, KVH, HD)
    row_steps = jnp.arange(BLOCK, dtype=jnp.int32)
    global_rows = jnp.concatenate([lax.dynamic_slice_in_dim(kv_seq, (global_ids[global_slot] * BLOCK).astype(jnp.int32), BLOCK, 0) for global_slot in range(GLOBALS)], axis=0)
    global_pos = (global_ids[:, None] * BLOCK + row_steps[None, :]).reshape(-1).astype(jnp.int32)
    head_index = jnp.arange(KVH, dtype=jnp.int32)

    def one_block(block_id):
        first_row = (block_id * BLOCK).astype(jnp.int32)
        query_rows = lax.dynamic_slice_in_dim(query_seq, first_row, BLOCK, 0).astype(jnp.float32)
        query_rows = query_rows.reshape(BLOCK, KVH, GROUP, HD)
        window_rows = lax.dynamic_slice_in_dim(padded, first_row, 3 * BLOCK, 0)
        window_pos = first_row - BLOCK + jnp.arange(3 * BLOCK, dtype=jnp.int32)
        shared_rows = jnp.concatenate([window_rows, global_rows], axis=0)
        shared_pos = jnp.concatenate([window_pos, global_pos])
        shared_heads = jnp.transpose(shared_rows.reshape(-1, 2, KVH, HD), (2, 0, 1, 3))
        own_lists = block_lists[block_id]
        random_heads = blocked[own_lists, :, :, head_index[:, None]].reshape(KVH, RAND * BLOCK, 2, HD)
        all_heads = jnp.concatenate([jnp.broadcast_to(shared_heads, (KVH,) + shared_heads.shape[1:]), random_heads], axis=1).astype(jnp.float32)
        random_pos = (own_lists[:, :, None] * BLOCK + row_steps).reshape(KVH, -1).astype(jnp.int32)
        query_doc = doc_index(doc_ends, first_row + row_steps)
        shared_ok = (shared_pos >= 0) & (shared_pos < LEN)
        shared_ok = shared_ok[None, :] & (doc_index(doc_ends, shared_pos)[None, :] == query_doc[:, None])
        random_ok = doc_index(doc_ends, random_pos)[:, None, :] == query_doc[None, :, None]
        allowed = jnp.concatenate([jnp.broadcast_to(shared_ok, (KVH,) + shared_ok.shape), random_ok], axis=2)
        result = attend_block(query_rows, all_heads[:, :, 0], all_heads[:, :, 1], allowed)
        return result.reshape(BLOCK, HEADS * HD)
    outputs = lax.map(one_block, jnp.arange(NBLK, dtype=jnp.int32))
    return outputs.reshape(LEN, HEADS * HD)

def reference(queries, keys_values, random_blocks, global_blocks, doc_lengths, cotangent):

    def one_sequence(seq_id):
        doc_ends = jnp.cumsum(doc_lengths[seq_id]).astype(jnp.int32)
        previous = jnp.zeros((LEN, HEADS * HD), jnp.float32)
        streams = []
        gradient_terms = []
        for section_id in range(SECTIONS):
            attention = section_attention(queries[section_id, seq_id], keys_values[section_id, seq_id], random_blocks[seq_id], global_blocks[seq_id], doc_ends)
            attention = lax.optimization_barrier(attention.astype(jnp.bfloat16)).astype(jnp.float32)
            if section_id == 0:
                handed = attention.astype(jnp.bfloat16)
            else:
                handed = (previous + attention).astype(jnp.bfloat16)
            widened = handed.astype(jnp.float32)
            previous = widened
            inverse = lax.rsqrt(lax.optimization_barrier(jnp.mean(widened * widened, axis=-1, keepdims=True)) + 1e-06)
            gradient_terms.append(lax.optimization_barrier(jnp.sum(cotangent[section_id, seq_id].astype(jnp.float32) * widened * inverse, axis=0)))
            streams.append(handed)
        return (jnp.stack(streams), jnp.stack(gradient_terms))
    stream, gradient_terms = lax.map(one_sequence, jnp.arange(SEQS, dtype=jnp.int32))
    return (jnp.transpose(stream, (1, 0, 2, 3)), lax.optimization_barrier(jnp.sum(gradient_terms, axis=0)) / SEQS)
```

```python
import functools
import math

import jax
import jax.numpy as jnp
from jax import lax
from jax.experimental import pallas as pl
from jax.experimental.pallas import tpu as pltpu
from jax.sharding import PartitionSpec as P

HEADS = 32
KVH = 4
HD = 128
RAND = 4
GLOBALS = 2
GROUP = 8
PART = 2
PARTS = KVH // PART
NEVER = -1e30
SCALE = math.log2(math.e) / math.sqrt(HD)
VMEM = pl.BlockSpec(memory_space=pltpu.VMEM)
SMEM = pl.BlockSpec(memory_space=pltpu.SMEM)


def count_docs(doc_ends, positions):
    found = jnp.zeros(positions.shape, jnp.int32)
    for end in doc_ends:
        found += (positions >= end).astype(jnp.int32)
    return found


def attend_kernel(part, place_ref, lists_ref, globals_ref, docs_ref, q_ref, *refs):
    kv_refs, out_ref = refs[:-1], refs[-1]
    rows = q_ref.shape[0]
    place = place_ref[0]
    doc_ends, end = [], 0
    for doc in range(docs_ref.shape[1]):
        end = end + docs_ref[0, doc]
        doc_ends.append(end)
    query_doc = count_docs(doc_ends, place * rows + lax.broadcasted_iota(jnp.int32, (rows, 1), 0))
    blocks, same = [], []
    for slot in range(len(kv_refs)):
        block = place ^ slot
        key_doc = count_docs(doc_ends, block * rows + lax.broadcasted_iota(jnp.int32, (1, rows), 1))
        blocks.append(block)
        same.append(query_doc == key_doc)
    for index in range(PART):
        head = part * PART + index
        biases = []
        for block, same_doc in zip(blocks, same):
            times = (jnp.abs(block - place) <= 1).astype(jnp.int32)
            for slot in range(GLOBALS):
                times += (globals_ref[0, slot] == block).astype(jnp.int32)
            for slot in range(RAND):
                times += (lists_ref[0, place, head, slot] == block).astype(jnp.int32)
            level = jnp.log2(jnp.full((1, rows), times, jnp.int32).astype(jnp.float32))
            biases.append(jnp.where(same_doc & (times > 0), level, NEVER))
        bias = jnp.concatenate(biases, axis=1)
        bias = jnp.concatenate([bias, bias], axis=0)
        keys = jnp.concatenate([ref[:, pl.ds(index * HD, HD)] for ref in kv_refs], axis=0)
        values = jnp.concatenate([ref[:, pl.ds((PART + index) * HD, HD)] for ref in kv_refs], axis=0)
        values = jnp.concatenate([values, jnp.ones_like(values)], axis=1)
        for pair in range(GROUP // 2):
            first = (index * GROUP + 2 * pair) * HD
            query = jnp.concatenate(
                [q_ref[:, pl.ds(first, HD)], q_ref[:, pl.ds(first + HD, HD)]], axis=0
            )
            scores = lax.dot_general(
                query, keys, (((1,), (1,)), ((), ())), preferred_element_type=jnp.float32
            )
            scores = scores * SCALE + bias
            weights = jnp.exp2(scores - jnp.max(scores, axis=1, keepdims=True))
            product = jnp.dot(
                weights.astype(jnp.bfloat16), values, preferred_element_type=jnp.float32
            )
            result = (product[:, :HD] / product[:, HD:]).astype(jnp.bfloat16)
            out_ref[:, pl.ds(first, HD)] = result[:rows]
            out_ref[:, pl.ds(first + HD, HD)] = result[rows:]


def attend(part, scalars, queries, kv_slots):
    rows = queries.shape[0]
    width = PART * GROUP * HD
    keys = rows * len(kv_slots)
    return pl.pallas_call(
        functools.partial(attend_kernel, part),
        out_shape=jax.ShapeDtypeStruct((rows, width), jnp.bfloat16),
        grid=(1,),
        in_specs=[SMEM] * 4
        + [pl.BlockSpec((rows, width), lambda step: (0, part))]
        + [VMEM] * len(kv_slots),
        out_specs=VMEM,
        compiler_params=pltpu.CompilerParams(vmem_limit_bytes=40 << 20),
        cost_estimate=pl.CostEstimate(
            flops=4 * rows * width * keys,
            bytes_accessed=4 * rows * width + 4 * keys * PART * HD,
            transcendentals=rows * PART * GROUP * keys,
        ),
        name="attend",
    )(*scalars, queries, *kv_slots)


def finish_kernel(scale, last_ref, cotangent_ref, *refs):
    arrived_refs, handed_refs = refs[:PARTS], refs[PARTS : 2 * PARTS]
    stream_ref, share_ref = refs[2 * PARTS :]
    rows, width = handed_refs[0].shape
    is_last = last_ref[0] == 1
    squares = jnp.zeros((rows, HD), jnp.float32)
    for part in range(PARTS):
        for column in range(0, width, HD):
            handed = handed_refs[part][:, pl.ds(column, HD)].astype(jnp.float32)
            arrived = arrived_refs[part][:, pl.ds(column, HD)].astype(jnp.float32)
            total = jnp.where(is_last, handed + arrived, handed).astype(jnp.bfloat16)
            stream_ref[:, pl.ds(part * width + column, HD)] = total
            widened = total.astype(jnp.float32)
            squares += widened * widened
    mean = jnp.sum(squares, axis=1, keepdims=True) / (PARTS * width)
    inverse = lax.rsqrt(mean + 1e-06) * scale
    for tile in range(PARTS * width // HD):
        columns = pl.ds(tile * HD, HD)
        term = cotangent_ref[:, columns].astype(jnp.float32) * stream_ref[:, columns].astype(jnp.float32)
        share_ref[pl.ds(tile, 1), :] = jnp.sum(term * inverse, axis=0, keepdims=True)


def finish(is_last, cotangent, arrived, handed, scale):
    rows, features = cotangent.shape
    return pl.pallas_call(
        functools.partial(finish_kernel, scale),
        out_shape=(
            jax.ShapeDtypeStruct((rows, features), jnp.bfloat16),
            jax.ShapeDtypeStruct((features // HD, HD), jnp.float32),
        ),
        in_specs=[SMEM] + [VMEM] * (1 + 2 * PARTS),
        out_specs=(VMEM, VMEM),
        compiler_params=pltpu.CompilerParams(vmem_limit_bytes=40 << 20),
        cost_estimate=pl.CostEstimate(
            flops=10 * rows * features, bytes_accessed=8 * rows * features, transcendentals=rows
        ),
        name="finish",
    )(is_last, cotangent, *arrived, *handed)


def swapped_sum(value, axis):
    count = lax.axis_size(axis)
    distance = 1
    while distance < count:
        value = value + lax.ppermute(value, axis, [(place, place ^ distance) for place in range(count)])
        distance *= 2
    return value


def gather_slots(value):
    count = lax.axis_size("ctx")
    slots = [value]
    for slot in range(1, count):
        pairs = [
            (place, place ^ slot)
            for place in range(count)
            if abs(place - (place ^ slot)) <= count // 2
        ]
        slots.append(lax.ppermute(value, "ctx", pairs))
    return slots


def per_device(queries, keys_values, random_blocks, global_blocks, doc_lengths, cotangent):
    queries, keys_values, cotangent = queries[0, 0], keys_values[0, 0], cotangent[0, 0]
    place = lax.axis_index("ctx").astype(jnp.int32).reshape(1)
    scalars = (place, random_blocks, global_blocks, doc_lengths)
    section_count = lax.axis_size("section")
    section_place = lax.axis_index("section")
    half = KVH * HD
    step_width = PART * HD
    slots = []
    for part in range(PARTS):
        first = part * step_width
        kv = jnp.concatenate(
            [
                keys_values[:, first : first + step_width],
                keys_values[:, half + first : half + first + step_width],
            ],
            axis=1,
        )
        slots.append(gather_slots(kv))
    handed, arrived = [], []
    for part in range(PARTS):
        handed.append(attend(part, scalars, queries, slots[part]))
        arrived.append(lax.ppermute(handed[part], "section", [(0, 1), (1, 0)]))
    for step in range(2, section_count):
        on_step = section_place == step - 1
        for part in range(PARTS):
            total = handed[part].astype(jnp.float32) + arrived[part].astype(jnp.float32)
            handed[part] = jnp.where(on_step, total.astype(jnp.bfloat16), handed[part])
            arrived[part] = lax.ppermute(handed[part], "section", [(step - 1, step), (step, step - 1)])
    is_last = (section_place == section_count - 1).astype(jnp.int32).reshape(1)
    stream, share = finish(is_last, cotangent, arrived, handed, 1.0 / lax.axis_size("dp"))
    gain_grad = swapped_sum(swapped_sum(share, "dp"), "ctx")
    return (stream[None, None], gain_grad.reshape(1, HEADS * HD))


def solution(mesh):
    in_specs = (
        P("section", "dp", "ctx", None),
        P("section", "dp", "ctx", None),
        P("dp", None, None, None),
        P("dp", None),
        P("dp", None),
        P("section", "dp", "ctx", None),
    )
    out_specs = (P("section", "dp", "ctx", None), P("section", None))
    return jax.shard_map(
        per_device, mesh=mesh, in_specs=in_specs, out_specs=out_specs, check_vma=False
    )
```

```python
import functools
import math

import jax
import jax.numpy as jnp
from jax import lax
from jax.experimental import pallas as pl
from jax.experimental.pallas import tpu as pltpu
from jax.sharding import PartitionSpec as P

HEADS = 32
KVH = 4
HD = 128
RAND = 4
GLOBALS = 2
GROUP = 8
PART = 2
PARTS = KVH // PART
NEVER = -1e30
SCALE = math.log2(math.e) / math.sqrt(HD)
VMEM = pl.BlockSpec(memory_space=pltpu.VMEM)
SMEM = pl.BlockSpec(memory_space=pltpu.SMEM)


def count_docs(doc_ends, positions):
    found = jnp.zeros(positions.shape, jnp.int32)
    for end in doc_ends:
        found += (positions >= end).astype(jnp.int32)
    return found


def attend_kernel(part, base, place_ref, lists_ref, globals_ref, docs_ref, q_ref, *refs):
    kv_refs, out_ref = refs[:-1], refs[-1]
    rows = q_ref.shape[0]
    place = place_ref[0]
    doc_ends, end = [], 0
    for doc in range(docs_ref.shape[1]):
        end = end + docs_ref[0, doc]
        doc_ends.append(end)
    query_doc = count_docs(doc_ends, place * rows + lax.broadcasted_iota(jnp.int32, (rows, 1), 0))
    blocks, same = [], []
    for slot in range(len(kv_refs)):
        block = place ^ slot
        key_doc = count_docs(doc_ends, block * rows + lax.broadcasted_iota(jnp.int32, (1, rows), 1))
        blocks.append(block)
        same.append(query_doc == key_doc)
    for index in range(PART):
        head = part * PART + index
        biases = []
        for block, same_doc in zip(blocks, same):
            times = (jnp.abs(block - place) <= 1).astype(jnp.int32)
            for slot in range(GLOBALS):
                times += (globals_ref[0, slot] == block).astype(jnp.int32)
            for slot in range(RAND):
                times += (lists_ref[0, place, head, slot] == block).astype(jnp.int32)
            level = jnp.log2(jnp.full((1, rows), times, jnp.int32).astype(jnp.float32))
            biases.append(jnp.where(same_doc & (times > 0), level, NEVER))
        bias = jnp.concatenate(biases, axis=1)
        bias = jnp.concatenate([bias, bias], axis=0)
        keys = jnp.concatenate([ref[:, pl.ds(base + index * HD, HD)] for ref in kv_refs], axis=0)
        values = jnp.concatenate([ref[:, pl.ds(base + (PART + index) * HD, HD)] for ref in kv_refs], axis=0)
        values = jnp.concatenate([values, jnp.ones_like(values)], axis=1)
        for pair in range(GROUP // 2):
            first = (index * GROUP + 2 * pair) * HD
            query = jnp.concatenate(
                [q_ref[:, pl.ds(first, HD)], q_ref[:, pl.ds(first + HD, HD)]], axis=0
            )
            scores = lax.dot_general(
                query, keys, (((1,), (1,)), ((), ())), preferred_element_type=jnp.float32
            )
            scores = scores * SCALE + bias
            weights = jnp.exp2(scores - jnp.max(scores, axis=1, keepdims=True))
            product = jnp.dot(
                weights.astype(jnp.bfloat16), values, preferred_element_type=jnp.float32
            )
            result = (product[:, :HD] / product[:, HD:]).astype(jnp.bfloat16)
            out_ref[:, pl.ds(first, HD)] = result[:rows]
            out_ref[:, pl.ds(first + HD, HD)] = result[rows:]


def prepare_kernel(queries_ref, kv_ref, *refs):
    for part in range(PARTS):
        width = PART * HD
        for side in range(2):
            source = pl.ds(side * KVH * HD + part * width, width)
            refs[part][:, pl.ds(side * width, width)] = kv_ref[:, source]
    refs[PARTS][...] = queries_ref[...]


def prepare(queries, keys_values):
    rows = queries.shape[0]
    width = PART * GROUP * HD
    outs = pl.pallas_call(
        prepare_kernel,
        grid=(1,),
        out_shape=[jax.ShapeDtypeStruct((rows, 2 * PART * HD), jnp.bfloat16)] * PARTS
        + [jax.ShapeDtypeStruct((rows, width), jnp.bfloat16)],
        in_specs=[pl.BlockSpec((rows, width), lambda step: (0, 0)), VMEM],
        out_specs=[VMEM] * (PARTS + 1),
        name="prepare",
    )(queries, keys_values)
    return outs[:PARTS], outs[PARTS]


def attend(part, scalars, queries, query_part, kv_slots, base):
    rows = queries.shape[0]
    width = PART * GROUP * HD
    keys = rows * len(kv_slots)
    return pl.pallas_call(
        functools.partial(attend_kernel, part, base),
        out_shape=jax.ShapeDtypeStruct((rows, width), jnp.bfloat16),
        grid=(1,),
        in_specs=[SMEM] * 4
        + [pl.BlockSpec((rows, width), lambda step: (0, query_part))]
        + [VMEM] * len(kv_slots),
        out_specs=VMEM,
        compiler_params=pltpu.CompilerParams(vmem_limit_bytes=40 << 20),
        cost_estimate=pl.CostEstimate(
            flops=120 * rows * width * keys,
            bytes_accessed=4 * rows * width + 4 * keys * PART * HD,
            transcendentals=rows * PART * GROUP * keys,
        ),
        name="attend",
    )(*scalars, queries, *kv_slots)


def finish_kernel(scale, last_ref, cotangent_ref, *refs):
    arrived_refs, handed_refs = refs[:PARTS], refs[PARTS : 2 * PARTS]
    stream_ref, share_ref = refs[2 * PARTS :]
    rows, width = handed_refs[0].shape
    is_last = last_ref[0] == 1
    squares = jnp.zeros((rows, HD), jnp.float32)
    for part in range(PARTS):
        for column in range(0, width, HD):
            handed = handed_refs[part][:, pl.ds(column, HD)].astype(jnp.float32)
            arrived = arrived_refs[part][:, pl.ds(column, HD)].astype(jnp.float32)
            total = jnp.where(is_last, handed + arrived, handed).astype(jnp.bfloat16)
            stream_ref[:, pl.ds(part * width + column, HD)] = total
            widened = total.astype(jnp.float32)
            squares += widened * widened
    mean = jnp.sum(squares, axis=1, keepdims=True) / (PARTS * width)
    inverse = lax.rsqrt(mean + 1e-06) * scale
    for tile in range(PARTS * width // HD):
        columns = pl.ds(tile * HD, HD)
        term = cotangent_ref[:, columns].astype(jnp.float32) * stream_ref[:, columns].astype(jnp.float32)
        share_ref[pl.ds(tile, 1), :] = jnp.sum(term * inverse, axis=0, keepdims=True)


def finish(is_last, cotangent, arrived, handed, scale):
    rows, features = cotangent.shape
    return pl.pallas_call(
        functools.partial(finish_kernel, scale),
        out_shape=(
            jax.ShapeDtypeStruct((rows, features), jnp.bfloat16),
            jax.ShapeDtypeStruct((features // HD, HD), jnp.float32),
        ),
        in_specs=[SMEM] + [VMEM] * (1 + 2 * PARTS),
        out_specs=(VMEM, VMEM),
        compiler_params=pltpu.CompilerParams(vmem_limit_bytes=40 << 20),
        cost_estimate=pl.CostEstimate(
            flops=10 * rows * features, bytes_accessed=8 * rows * features, transcendentals=rows
        ),
        name="finish",
    )(is_last, cotangent, *arrived, *handed)


def swapped_sum(value, axis):
    count = lax.axis_size(axis)
    distance = 1
    while distance < count:
        value = value + lax.ppermute(value, axis, [(place, place ^ distance) for place in range(count)])
        distance *= 2
    return value


def gather_slots(value, sections):
    count = lax.axis_size("ctx")
    slots = [value]
    for slot in range(1, count):
        pairs = [
            (section * count + place, section * count + (place ^ slot))
            for section in sections
            for place in range(count)
            if abs(place - (place ^ slot)) <= count // 2
        ]
        slots.append(lax.ppermute(value, ("section", "ctx"), pairs))
    return slots


def per_device(queries, keys_values, random_blocks, global_blocks, doc_lengths, cotangent):
    queries, keys_values, cotangent = queries[0, 0], keys_values[0, 0], cotangent[0, 0]
    place = lax.axis_index("ctx").astype(jnp.int32).reshape(1)
    scalars = (place, random_blocks, global_blocks, doc_lengths)
    section_count = lax.axis_size("section")
    section_place = lax.axis_index("section")
    parts, early_queries = prepare(queries, keys_values)
    every = range(section_count)
    first_hop = [(0, 1), (1, 0)]
    early_kv = lax.ppermute(parts[0], "section", first_hop)
    late_slots = gather_slots(parts[1], every)
    early_queries = lax.ppermute(early_queries, "section", first_hop)
    both = jnp.concatenate([parts[0], early_kv], axis=1)
    both, late_slots[1] = lax.optimization_barrier((both, late_slots[1]))
    both_slots = gather_slots(both, every)
    late = attend(1, scalars, queries, 1, late_slots, 0)
    arrived_late = lax.ppermute(late, "section", first_hop)
    own = attend(0, scalars, queries, 0, both_slots, 0)
    arrived = [attend(0, scalars, early_queries, 0, both_slots, parts[0].shape[1]), arrived_late]
    handed = [own, late]
    for step in range(2, section_count):
        on_step = section_place == step - 1
        for part in range(PARTS):
            total = handed[part].astype(jnp.float32) + arrived[part].astype(jnp.float32)
            handed[part] = jnp.where(on_step, total.astype(jnp.bfloat16), handed[part])
            arrived[part] = lax.ppermute(handed[part], "section", [(step - 1, step), (step, step - 1)])
    is_last = (section_place == section_count - 1).astype(jnp.int32).reshape(1)
    stream, share = finish(is_last, cotangent, arrived, handed, 1.0 / lax.axis_size("dp"))
    gain_grad = swapped_sum(swapped_sum(share, "dp"), "ctx")
    return (stream[None, None], gain_grad.reshape(1, HEADS * HD))


def solution(mesh):
    in_specs = (
        P("section", "dp", "ctx", None),
        P("section", "dp", "ctx", None),
        P("dp", None, None, None),
        P("dp", None),
        P("dp", None),
        P("section", "dp", "ctx", None),
    )
    out_specs = (P("section", "dp", "ctx", None), P("section", None))
    return jax.shard_map(
        per_device, mesh=mesh, in_specs=in_specs, out_specs=out_specs, check_vma=False
    )
```

```python
import functools
import math

import jax
import jax.numpy as jnp
from jax import lax
from jax.experimental import pallas as pl
from jax.experimental.pallas import tpu as pltpu
from jax.sharding import PartitionSpec as P

HEADS = 32
KVH = 4
HD = 128
RAND = 4
GLOBALS = 2
GROUP = 8
PART = 2
PARTS = KVH // PART
NEVER = -1e30
LEVELS = 8
SCALE = math.log2(math.e) / math.sqrt(HD)
VMEM = pl.BlockSpec(memory_space=pltpu.VMEM)
SMEM = pl.BlockSpec(memory_space=pltpu.SMEM)


def count_docs(doc_ends, positions):
    found = jnp.zeros(positions.shape, jnp.int32)
    for end in doc_ends:
        found += (positions >= end).astype(jnp.int32)
    return found


def weigh_kernel(place_ref, lists_ref, globals_ref, docs_ref, out_ref):
    rows, width = out_ref.shape[0] - LEVELS, out_ref.shape[1]
    place = place_ref[0]
    doc_ends, end = [], 0
    for doc in range(docs_ref.shape[1]):
        end = end + docs_ref[0, doc]
        doc_ends.append(end)
    query_doc = count_docs(doc_ends, place * rows + lax.broadcasted_iota(jnp.int32, (rows, 1), 0))
    for slot in range(width // rows):
        block = place ^ slot
        columns = pl.ds(slot * rows, rows)
        key_doc = count_docs(doc_ends, block * rows + lax.broadcasted_iota(jnp.int32, (1, rows), 1))
        out_ref[pl.ds(0, rows), columns] = jnp.where(query_doc == key_doc, 0.0, NEVER)
        shared = (jnp.abs(block - place) <= 1).astype(jnp.int32)
        for entry in range(GLOBALS):
            shared += (globals_ref[0, entry] == block).astype(jnp.int32)
        for head in range(KVH):
            times = shared
            for entry in range(RAND):
                times += (lists_ref[0, place, head, entry] == block).astype(jnp.int32)
            times = jnp.full((1, rows), times, jnp.int32)
            level = jnp.where(times > 0, jnp.log2(times.astype(jnp.float32)), NEVER)
            out_ref[pl.ds(rows + head, 1), columns] = level


def weigh(scalars, rows, slots):
    return pl.pallas_call(
        weigh_kernel,
        out_shape=jax.ShapeDtypeStruct((rows + LEVELS, slots * rows), jnp.float32),
        in_specs=[SMEM] * 4,
        out_specs=VMEM,
        compiler_params=pltpu.CompilerParams(vmem_limit_bytes=16 << 20),
        name="weigh",
    )(*scalars)


def attend_kernel(part, base, weights_ref, q_ref, *refs):
    kv_refs, out_ref = refs[:-1], refs[-1]
    rows = q_ref.shape[0]
    for index in range(PART):
        bias = weights_ref[pl.ds(0, rows), :] + weights_ref[pl.ds(rows + part * PART + index, 1), :]
        bias = jnp.concatenate([bias, bias], axis=0)
        keys = jnp.concatenate([ref[:, pl.ds(base + index * HD, HD)] for ref in kv_refs], axis=0)
        values = jnp.concatenate([ref[:, pl.ds(base + (PART + index) * HD, HD)] for ref in kv_refs], axis=0)
        values = jnp.concatenate([values, jnp.ones_like(values)], axis=1)
        for pair in range(GROUP // 2):
            first = (index * GROUP + 2 * pair) * HD
            query = jnp.concatenate(
                [q_ref[:, pl.ds(first, HD)], q_ref[:, pl.ds(first + HD, HD)]], axis=0
            )
            scores = lax.dot_general(
                query, keys, (((1,), (1,)), ((), ())), preferred_element_type=jnp.float32
            )
            scores = scores * SCALE + bias
            weights = jnp.exp2(scores - jnp.max(scores, axis=1, keepdims=True))
            product = jnp.dot(
                weights.astype(jnp.bfloat16), values, preferred_element_type=jnp.float32
            )
            result = (product[:, :HD] / product[:, HD:]).astype(jnp.bfloat16)
            out_ref[:, pl.ds(first, HD)] = result[:rows]
            out_ref[:, pl.ds(first + HD, HD)] = result[rows:]


def attend(part, weights, queries, query_part, kv_slots, base=0):
    rows = queries.shape[0]
    width = PART * GROUP * HD
    keys = rows * len(kv_slots)
    return pl.pallas_call(
        functools.partial(attend_kernel, part, base),
        grid=(1,),
        out_shape=jax.ShapeDtypeStruct((rows, width), jnp.bfloat16),
        in_specs=[
            VMEM,
            pl.BlockSpec((rows, width), lambda step: (0, query_part)),
        ]
        + [VMEM] * len(kv_slots),
        out_specs=VMEM,
        compiler_params=pltpu.CompilerParams(vmem_limit_bytes=40 << 20),
        cost_estimate=pl.CostEstimate(
            flops=120 * rows * width * keys,
            bytes_accessed=4 * rows * width + 4 * keys * PART * HD,
            transcendentals=rows * PART * GROUP * keys,
        ),
        name="attend",
    )(weights, queries, *kv_slots)


def finish_kernel(scale, last_ref, cotangent_ref, *refs):
    arrived_refs, handed_refs = refs[:PARTS], refs[PARTS : 2 * PARTS]
    stream_ref, share_ref = refs[2 * PARTS :]
    rows, width = handed_refs[0].shape
    is_last = last_ref[0] == 1
    squares = jnp.zeros((rows, HD), jnp.float32)
    for part in range(PARTS):
        for column in range(0, width, HD):
            handed = handed_refs[part][:, pl.ds(column, HD)].astype(jnp.float32)
            arrived = arrived_refs[part][:, pl.ds(column, HD)].astype(jnp.float32)
            total = jnp.where(is_last, handed + arrived, handed).astype(jnp.bfloat16)
            stream_ref[:, pl.ds(part * width + column, HD)] = total
            widened = total.astype(jnp.float32)
            squares += widened * widened
    mean = jnp.sum(squares, axis=1, keepdims=True) / (PARTS * width)
    inverse = lax.rsqrt(mean + 1e-06) * scale
    for tile in range(PARTS * width // HD):
        columns = pl.ds(tile * HD, HD)
        term = cotangent_ref[:, columns].astype(jnp.float32) * stream_ref[:, columns].astype(jnp.float32)
        share_ref[pl.ds(tile, 1), :] = jnp.sum(term * inverse, axis=0, keepdims=True)


def finish(is_last, cotangent, arrived, handed, scale):
    rows, features = cotangent.shape
    return pl.pallas_call(
        functools.partial(finish_kernel, scale),
        out_shape=(
            jax.ShapeDtypeStruct((rows, features), jnp.bfloat16),
            jax.ShapeDtypeStruct((features // HD, HD), jnp.float32),
        ),
        in_specs=[SMEM] + [VMEM] * (1 + 2 * PARTS),
        out_specs=(VMEM, VMEM),
        compiler_params=pltpu.CompilerParams(vmem_limit_bytes=40 << 20),
        cost_estimate=pl.CostEstimate(
            flops=10 * rows * features, bytes_accessed=8 * rows * features, transcendentals=rows
        ),
        name="finish",
    )(is_last, cotangent, *arrived, *handed)


def swapped_sum(value, axis, distances):
    count = lax.axis_size(axis)
    for distance in distances:
        value = value + lax.ppermute(value, axis, [(place, place ^ distance) for place in range(count)])
    return value


def powers(first, end):
    return [1 << step for step in range(first, (end - 1).bit_length())]


def total_share(value):
    replicas, count = lax.axis_size("dp"), lax.axis_size("ctx")
    value = swapped_sum(value, "dp", [1])
    if replicas != 4 or count > 4:
        return swapped_sum(swapped_sum(value, "dp", powers(1, replicas)), "ctx", powers(0, count))
    core = lax.axis_index("dp") % 2
    heard = []
    for distance in range(count):
        pairs = []
        for replica in range(replicas):
            for place in range(count):
                across = replica ^ 2 if distance == 0 or replica % 2 else replica
                pairs.append((replica * count + place, across * count + (place ^ distance)))
        heard.append(lax.ppermute(value, ("dp", "ctx"), pairs))
    value = sum(heard[1:], jnp.where(core == 0, value + heard[0], 0.0))
    return swapped_sum(value, "dp", [1])


def gather_slots(value):
    count, replicas = lax.axis_size("ctx"), lax.axis_size("dp")
    slots = [value]
    for slot in range(1, count):
        pairs = []
        for replica in range(replicas):
            for place in range(count):
                near = abs(place - (place ^ slot)) <= count // 2
                partner = (replica, place ^ slot) if near else (replica ^ 1, place)
                pairs.append((replica * count + place, partner[0] * count + partner[1]))
        slots.append(lax.ppermute(value, ("dp", "ctx"), pairs))
    return slots


def per_device(queries, keys_values, random_blocks, global_blocks, doc_lengths, cotangent):
    queries, keys_values, cotangent = queries[0, 0], keys_values[0, 0], cotangent[0, 0]
    place = lax.axis_index("ctx").astype(jnp.int32).reshape(1)
    scalars = (place, random_blocks, global_blocks, doc_lengths)
    section_count = lax.axis_size("section")
    section_place = lax.axis_index("section")
    half = KVH * HD
    kv_width = PART * HD
    parts = []
    for part in range(PARTS):
        first = part * kv_width
        parts.append(
            jnp.concatenate(
                [
                    keys_values[:, first : first + kv_width],
                    keys_values[:, half + first : half + first + kv_width],
                ],
                axis=1,
            )
        )
    weights = weigh(scalars, queries.shape[0], lax.axis_size("ctx"))
    first_hop = [(0, 1), (1, 0)]
    early_kv = lax.ppermute(parts[0], "section", first_hop)
    late_slots = gather_slots(parts[1])
    early_queries = lax.ppermute(queries[:, : PART * GROUP * HD], "section", first_hop)
    own_kv, late_slots[1] = lax.optimization_barrier((parts[0], late_slots[1]))
    own_slots = gather_slots(own_kv)
    late = attend(1, weights, queries, 1, late_slots)
    arrived_late = lax.ppermute(late, "section", first_hop)
    early_kv, own_slots[1] = lax.optimization_barrier((early_kv, own_slots[1]))
    early_slots = gather_slots(early_kv)
    own = attend(0, weights, queries, 0, own_slots)
    arrived = [attend(0, weights, early_queries, 0, early_slots), arrived_late]
    handed = [own, late]
    for step in range(2, section_count):
        on_step = section_place == step - 1
        for part in range(PARTS):
            total = handed[part].astype(jnp.float32) + arrived[part].astype(jnp.float32)
            handed[part] = jnp.where(on_step, total.astype(jnp.bfloat16), handed[part])
            arrived[part] = lax.ppermute(handed[part], "section", [(step - 1, step), (step, step - 1)])
    is_last = (section_place == section_count - 1).astype(jnp.int32).reshape(1)
    stream, share = finish(is_last, cotangent, arrived, handed, 1.0 / lax.axis_size("dp"))
    gain_grad = total_share(share)
    return (stream[None, None], gain_grad.reshape(1, HEADS * HD))


def solution(mesh):
    in_specs = (
        P("section", "dp", "ctx", None),
        P("section", "dp", "ctx", None),
        P("dp", None, None, None),
        P("dp", None),
        P("dp", None),
        P("section", "dp", "ctx", None),
    )
    out_specs = (P("section", "dp", "ctx", None), P("section", None))
    return jax.shard_map(
        per_device, mesh=mesh, in_specs=in_specs, out_specs=out_specs, check_vma=False
    )
```

```python
import functools
import math

import jax
import jax.numpy as jnp
from jax import lax
from jax.experimental import pallas as pl
from jax.experimental.pallas import tpu as pltpu
from jax.sharding import PartitionSpec as P

HEADS = 32
KVH = 4
HD = 128
RAND = 4
GLOBALS = 2
GROUP = 8
EARLY = 2
GROUPS = (range(EARLY), range(EARLY, KVH))
PARTS = len(GROUPS)
NEVER = -1e30
LEVELS = 8
SCALE = math.log2(math.e) / math.sqrt(HD)
VMEM = pl.BlockSpec(memory_space=pltpu.VMEM)
SMEM = pl.BlockSpec(memory_space=pltpu.SMEM)
ANY = pl.BlockSpec(memory_space=pl.ANY)


def count_docs(doc_ends, positions):
    found = jnp.zeros(positions.shape, jnp.int32)
    for end in doc_ends:
        found += (positions >= end).astype(jnp.int32)
    return found


def weigh_kernel(place_ref, lists_ref, globals_ref, docs_ref, out_ref):
    rows, width = out_ref.shape[0] - LEVELS, out_ref.shape[1]
    place = place_ref[0]
    doc_ends, end = [], 0
    for doc in range(docs_ref.shape[1]):
        end = end + docs_ref[0, doc]
        doc_ends.append(end)
    query_doc = count_docs(doc_ends, place * rows + lax.broadcasted_iota(jnp.int32, (rows, 1), 0))
    for slot in range(width // rows):
        block = place ^ slot
        columns = pl.ds(slot * rows, rows)
        key_doc = count_docs(doc_ends, block * rows + lax.broadcasted_iota(jnp.int32, (1, rows), 1))
        out_ref[pl.ds(0, rows), columns] = jnp.where(query_doc == key_doc, 0.0, NEVER)
        shared = (jnp.abs(block - place) <= 1).astype(jnp.int32)
        for entry in range(GLOBALS):
            shared += (globals_ref[0, entry] == block).astype(jnp.int32)
        for head in range(KVH):
            times = shared
            for entry in range(RAND):
                times += (lists_ref[0, place, head, entry] == block).astype(jnp.int32)
            times = jnp.full((1, rows), times, jnp.int32)
            level = jnp.where(times > 0, jnp.log2(times.astype(jnp.float32)), NEVER)
            out_ref[pl.ds(rows + head, 1), columns] = level


def weigh(scalars, rows, slots):
    return pl.pallas_call(
        weigh_kernel,
        out_shape=jax.ShapeDtypeStruct((rows + LEVELS, slots * rows), jnp.float32),
        in_specs=[SMEM] * 4,
        out_specs=VMEM,
        compiler_params=pltpu.CompilerParams(vmem_limit_bytes=16 << 20),
        name="weigh",
    )(*scalars)


def attend_kernel(heads, key_base, value_base, place_ref, weights_ref, q_ref, *refs):
    kv_refs, out_ref = refs[:-1], refs[-1]
    rows = q_ref.shape[0]
    slots = weights_ref.shape[1] // rows
    at_end = (place_ref[0] == 0) | (place_ref[0] == slots - 1)

    def blocks(column):
        found = [ref[:, pl.ds(column, HD)] for ref in kv_refs]
        if len(found) > slots:
            found[2] = jnp.where(at_end, found[slots], found[2])
        return jnp.concatenate(found[:slots], axis=0)

    for index, head in enumerate(heads):
        bias = weights_ref[pl.ds(0, rows), :] + weights_ref[pl.ds(rows + head, 1), :]
        bias = jnp.concatenate([bias, bias], axis=0)
        keys = blocks(key_base + index * HD)
        values = blocks(value_base + index * HD)
        values = jnp.concatenate([values, jnp.ones_like(values)], axis=1)
        for pair in range(GROUP // 2):
            first = (index * GROUP + 2 * pair) * HD
            query = jnp.concatenate(
                [q_ref[:, pl.ds(first, HD)], q_ref[:, pl.ds(first + HD, HD)]], axis=0
            )
            scores = lax.dot_general(
                query, keys, (((1,), (1,)), ((), ())), preferred_element_type=jnp.float32
            )
            scores = scores * SCALE + bias
            weights = jnp.exp2(scores - jnp.max(scores, axis=1, keepdims=True))
            product = jnp.dot(
                weights.astype(jnp.bfloat16), values, preferred_element_type=jnp.float32
            )
            result = (product[:, :HD] / product[:, HD:]).astype(jnp.bfloat16)
            out_ref[:, pl.ds(first, HD)] = result[:rows]
            out_ref[:, pl.ds(first + HD, HD)] = result[rows:]


def attend(heads, place, weights, queries, kv_slots, key_base, value_base, effort):
    rows, width = queries.shape
    keys = weights.shape[1]
    return pl.pallas_call(
        functools.partial(attend_kernel, heads, key_base, value_base),
        out_shape=jax.ShapeDtypeStruct((rows, width), jnp.bfloat16),
        in_specs=[SMEM] + [VMEM] * (2 + len(kv_slots)),
        out_specs=VMEM,
        compiler_params=pltpu.CompilerParams(vmem_limit_bytes=16 << 20),
        cost_estimate=pl.CostEstimate(
            flops=effort * rows * width * keys,
            bytes_accessed=4 * rows * width + 4 * keys * len(heads) * HD,
            transcendentals=rows * width * keys // HD,
        ),
        name="attend",
    )(place, weights, queries, *kv_slots)


def finish_kernel(scale, last_ref, cotangent_ref, *refs):
    arrived_refs, handed_refs = refs[:PARTS], refs[PARTS : 2 * PARTS]
    out_ref, share_ref, cotangent, stream, arrived_last, sems = refs[2 * PARTS :]
    rows, features = stream.shape
    last_copy = pltpu.make_async_copy(arrived_refs[-1], arrived_last, sems.at[0])
    last_copy.start()
    cotangent_copy = pltpu.make_async_copy(cotangent_ref, cotangent, sems.at[1])
    cotangent_copy.start()
    is_last = last_ref[0] == 1
    squares = jnp.zeros((rows, HD), jnp.float32)
    done = 0
    for part in range(PARTS):
        source = arrived_refs[part]
        if part == PARTS - 1:
            last_copy.wait()
            source = arrived_last
        for column in range(0, source.shape[1], HD):
            handed = handed_refs[part][:, pl.ds(column, HD)].astype(jnp.float32)
            arrived = source[:, pl.ds(column, HD)].astype(jnp.float32)
            total = jnp.where(is_last, handed + arrived, handed).astype(jnp.bfloat16)
            stream[:, pl.ds(done + column, HD)] = total
            widened = total.astype(jnp.float32)
            squares += widened * widened
        done += source.shape[1]
    store_copy = pltpu.make_async_copy(stream, out_ref, sems.at[2])
    store_copy.start()
    mean = jnp.sum(squares, axis=1, keepdims=True) / features
    inverse = lax.rsqrt(mean + 1e-06) * scale
    cotangent_copy.wait()
    for tile in range(features // HD):
        columns = pl.ds(tile * HD, HD)
        term = cotangent[:, columns].astype(jnp.float32) * stream[:, columns].astype(jnp.float32)
        share_ref[pl.ds(tile, 1), :] = jnp.sum(term * inverse, axis=0, keepdims=True)
    store_copy.wait()


def finish(is_last, cotangent, arrived, handed, scale):
    rows, features = cotangent.shape
    return pl.pallas_call(
        functools.partial(finish_kernel, scale),
        out_shape=(
            jax.ShapeDtypeStruct((rows, features), jnp.bfloat16),
            jax.ShapeDtypeStruct((features // HD, HD), jnp.float32),
        ),
        in_specs=[SMEM, ANY] + [VMEM] * (PARTS - 1) + [ANY] + [VMEM] * PARTS,
        out_specs=(ANY, VMEM),
        scratch_shapes=[
            pltpu.VMEM((rows, features), jnp.bfloat16),
            pltpu.VMEM((rows, features), jnp.bfloat16),
            pltpu.VMEM(arrived[-1].shape, jnp.bfloat16),
            pltpu.SemaphoreType.DMA((3,)),
        ],
        compiler_params=pltpu.CompilerParams(vmem_limit_bytes=16 << 20),
        cost_estimate=pl.CostEstimate(
            flops=10 * rows * features, bytes_accessed=8 * rows * features, transcendentals=rows
        ),
        name="finish",
    )(is_last, cotangent, *arrived, *handed)


def split_kernel(queries_ref, *out_refs):
    done = 0
    for out_ref in out_refs:
        out_ref[...] = queries_ref[:, pl.ds(done, out_ref.shape[1])]
        done += out_ref.shape[1]


def split(queries):
    rows = queries.shape[0]
    return pl.pallas_call(
        split_kernel,
        out_shape=[
            jax.ShapeDtypeStruct((rows, len(heads) * GROUP * HD), jnp.bfloat16) for heads in GROUPS
        ],
        in_specs=[VMEM],
        out_specs=[VMEM] * PARTS,
        compiler_params=pltpu.CompilerParams(vmem_limit_bytes=16 << 20),
        name="split",
    )(queries)


def swapped_sum(value, axis, distances):
    count = lax.axis_size(axis)
    for distance in distances:
        value = value + lax.ppermute(value, axis, [(place, place ^ distance) for place in range(count)])
    return value


def powers(first, end):
    return [1 << step for step in range(first, (end - 1).bit_length())]


def total_share(value):
    replicas, count = lax.axis_size("dp"), lax.axis_size("ctx")
    value = swapped_sum(value, "dp", [1])
    if replicas != 4 or count > 4:
        return swapped_sum(swapped_sum(value, "dp", powers(1, replicas)), "ctx", powers(0, count))
    core = lax.axis_index("dp") % 2
    heard = []
    for distance in range(count):
        pairs = []
        for replica in range(replicas):
            for place in range(count):
                across = replica ^ 2 if distance == 0 or replica % 2 else replica
                pairs.append((replica * count + place, across * count + (place ^ distance)))
        heard.append(lax.ppermute(value, ("dp", "ctx"), pairs))
    value = sum(heard[1:], jnp.where(core == 0, value + heard[0], 0.0))
    return swapped_sum(value, "dp", [1])


def fetch(value, slot):
    count, replicas = lax.axis_size("ctx"), lax.axis_size("dp")
    pairs = []
    for replica in range(replicas):
        for place in range(count):
            near = abs(place - (place ^ slot)) <= count // 2
            partner = (replica, place ^ slot) if near else (replica ^ 1, place)
            pairs.append((replica * count + place, partner[0] * count + partner[1]))
    return lax.ppermute(value, ("dp", "ctx"), pairs)


def gather_slots(value):
    return [value] + [fetch(value, slot) for slot in range(1, lax.axis_size("ctx"))]


def per_device(queries, keys_values, random_blocks, global_blocks, doc_lengths, cotangent):
    queries, keys_values, cotangent = queries[0, 0], keys_values[0, 0], cotangent[0, 0]
    place = lax.axis_index("ctx").astype(jnp.int32).reshape(1)
    scalars = (place, random_blocks, global_blocks, doc_lengths)
    section_count = lax.axis_size("section")
    section_place = lax.axis_index("section")
    half = KVH * HD
    early_width = EARLY * HD
    early_heads, late_heads = GROUPS
    weights = weigh(scalars, queries.shape[0], lax.axis_size("ctx"))
    first_hop = [(0, 1), (1, 0)]
    kv_parts = []
    for heads in GROUPS:
        first, last = heads[0] * HD, (heads[-1] + 1) * HD
        kv_parts.append(
            jnp.concatenate([keys_values[:, first:last], keys_values[:, half + first : half + last]], axis=1)
        )
    early_kv = lax.ppermute(kv_parts[0], "section", first_hop)
    late_slots = gather_slots(kv_parts[1])
    queries = list(split(queries))
    early_queries = lax.ppermute(queries[0], "section", first_hop)
    both = jnp.concatenate([kv_parts[0], early_kv], axis=1)
    late_slots[1], early_kv = lax.optimization_barrier((late_slots[1], early_kv))
    late = attend(late_heads, place, weights, queries[1], late_slots, 0, half - early_width, 120)
    arrived_late = lax.ppermute(late, "section", first_hop)
    if lax.axis_size("ctx") == 4:
        first, third = fetch(both, 1), fetch(both, 3)
        third, early_queries = lax.optimization_barrier((third, early_queries))
        both_slots = [both, first, fetch(first, 3), third, fetch(third, 1)]
    else:
        both_slots = gather_slots(both)
    own = attend(early_heads, place, weights, queries[0], both_slots, 0, early_width, 1)
    early = attend(
        early_heads, place, weights, early_queries, both_slots, 2 * early_width, 3 * early_width, 1
    )
    arrived = [early, arrived_late]
    handed = [own, late]
    for step in range(2, section_count):
        on_step = section_place == step - 1
        for part in range(PARTS):
            total = handed[part].astype(jnp.float32) + arrived[part].astype(jnp.float32)
            handed[part] = jnp.where(on_step, total.astype(jnp.bfloat16), handed[part])
            arrived[part] = lax.ppermute(handed[part], "section", [(step - 1, step), (step, step - 1)])
    is_last = (section_place == section_count - 1).astype(jnp.int32).reshape(1)
    stream, share = finish(is_last, cotangent, arrived, handed, 1.0 / lax.axis_size("dp"))
    gain_grad = total_share(share)
    return (stream[None, None], gain_grad.reshape(1, HEADS * HD))


def solution(mesh):
    in_specs = (
        P("section", "dp", "ctx", None),
        P("section", "dp", "ctx", None),
        P("dp", None, None, None),
        P("dp", None),
        P("dp", None),
        P("section", "dp", "ctx", None),
    )
    out_specs = (P("section", "dp", "ctx", None), P("section", None))
    return jax.shard_map(
        per_device, mesh=mesh, in_specs=in_specs, out_specs=out_specs, check_vma=False
    )
```

```python
import functools
import math

import jax
import jax.numpy as jnp
from jax import lax
from jax.experimental import pallas as pl
from jax.experimental.pallas import tpu as pltpu
from jax.sharding import PartitionSpec as P

HEADS = 32
KVH = 4
HD = 128
RAND = 4
GLOBALS = 2
GROUP = 8
EARLY = 2
GROUPS = (range(EARLY), range(EARLY, KVH))
PARTS = len(GROUPS)
NEVER = -1e30
LEVELS = 8
SCALE = math.log2(math.e) / math.sqrt(HD)
VMEM = pl.BlockSpec(memory_space=pltpu.VMEM)
SMEM = pl.BlockSpec(memory_space=pltpu.SMEM)
ANY = pl.BlockSpec(memory_space=pl.ANY)


def count_docs(doc_ends, positions):
    found = jnp.zeros(positions.shape, jnp.int32)
    for end in doc_ends:
        found += (positions >= end).astype(jnp.int32)
    return found


def weigh_kernel(place_ref, lists_ref, globals_ref, docs_ref, out_ref):
    rows, width = out_ref.shape[0] - LEVELS, out_ref.shape[1]
    place = place_ref[0]
    doc_ends, end = [], 0
    for doc in range(docs_ref.shape[1]):
        end = end + docs_ref[0, doc]
        doc_ends.append(end)
    query_doc = count_docs(doc_ends, place * rows + lax.broadcasted_iota(jnp.int32, (rows, 1), 0))
    for slot in range(width // rows):
        block = place ^ slot
        columns = pl.ds(slot * rows, rows)
        key_doc = count_docs(doc_ends, block * rows + lax.broadcasted_iota(jnp.int32, (1, rows), 1))
        out_ref[pl.ds(0, rows), columns] = jnp.where(query_doc == key_doc, 0.0, NEVER)
        shared = (jnp.abs(block - place) <= 1).astype(jnp.int32)
        for entry in range(GLOBALS):
            shared += (globals_ref[0, entry] == block).astype(jnp.int32)
        for head in range(KVH):
            times = shared
            for entry in range(RAND):
                times += (lists_ref[0, place, head, entry] == block).astype(jnp.int32)
            times = jnp.full((1, rows), times, jnp.int32)
            level = jnp.where(times > 0, jnp.log2(times.astype(jnp.float32)), NEVER)
            out_ref[pl.ds(rows + head, 1), columns] = level


def weigh(scalars, rows, slots):
    return pl.pallas_call(
        weigh_kernel,
        out_shape=jax.ShapeDtypeStruct((rows + LEVELS, slots * rows), jnp.float32),
        in_specs=[SMEM] * 4,
        out_specs=VMEM,
        compiler_params=pltpu.CompilerParams(vmem_limit_bytes=16 << 20),
        name="weigh",
    )(*scalars)


def attend_kernel(heads, query_base, key_base, value_base, kv_count, place_ref, weights_ref, q_ref, *refs):
    kv_refs, out_ref, scratch = refs[:kv_count], refs[kv_count], refs[kv_count + 1 :]
    rows = q_ref.shape[0]
    copies = []
    if scratch:
        for index in range(len(heads)):
            columns = pl.ds(index * GROUP * HD, GROUP * HD)
            source = q_ref.at[:, pl.ds(query_base + index * GROUP * HD, GROUP * HD)]
            copies.append(pltpu.make_async_copy(source, scratch[0].at[:, columns], scratch[1].at[index]))
            copies[-1].start()
        q_ref, query_base = scratch[0], 0
    slots = weights_ref.shape[1] // rows
    at_end = (place_ref[0] == 0) | (place_ref[0] == slots - 1)

    def blocks(column):
        found = [ref[:, pl.ds(column, HD)] for ref in kv_refs]
        if len(found) > slots:
            found[2] = jnp.where(at_end, found[slots], found[2])
        return jnp.concatenate(found[:slots], axis=0)

    for index, head in enumerate(heads):
        bias = weights_ref[pl.ds(0, rows), :] + weights_ref[pl.ds(rows + head, 1), :]
        bias = jnp.concatenate([bias, bias], axis=0)
        keys = blocks(key_base + index * HD)
        values = blocks(value_base + index * HD)
        values = jnp.concatenate([values, jnp.ones_like(values)], axis=1)
        if copies:
            copies[index].wait()
        for pair in range(GROUP // 2):
            first = (index * GROUP + 2 * pair) * HD
            source = query_base + first
            query = jnp.concatenate(
                [q_ref[:, pl.ds(source, HD)], q_ref[:, pl.ds(source + HD, HD)]], axis=0
            )
            scores = lax.dot_general(
                query, keys, (((1,), (1,)), ((), ())), preferred_element_type=jnp.float32
            )
            scores = scores * SCALE + bias
            weights = jnp.exp2(scores - jnp.max(scores, axis=1, keepdims=True))
            product = jnp.dot(
                weights.astype(jnp.bfloat16), values, preferred_element_type=jnp.float32
            )
            result = (product[:, :HD] / product[:, HD:]).astype(jnp.bfloat16)
            out_ref[:, pl.ds(first, HD)] = result[:rows]
            out_ref[:, pl.ds(first + HD, HD)] = result[rows:]


def attend(heads, place, weights, queries, query_base, kv_slots, key_base, value_base, effort, fetched=False):
    rows, width = queries.shape[0], len(heads) * GROUP * HD
    keys = weights.shape[1]
    return pl.pallas_call(
        functools.partial(attend_kernel, heads, query_base, key_base, value_base, len(kv_slots)),
        out_shape=jax.ShapeDtypeStruct((rows, width), jnp.bfloat16),
        in_specs=[SMEM, VMEM, ANY if fetched else VMEM] + [VMEM] * len(kv_slots),
        out_specs=VMEM,
        scratch_shapes=[
            pltpu.VMEM((rows, width), jnp.bfloat16),
            pltpu.SemaphoreType.DMA((len(heads),)),
        ]
        if fetched
        else [],
        compiler_params=pltpu.CompilerParams(vmem_limit_bytes=(16 if fetched else 16) << 20),
        cost_estimate=pl.CostEstimate(
            flops=effort * rows * width * keys,
            bytes_accessed=4 * rows * width + 4 * keys * len(heads) * HD,
            transcendentals=rows * width * keys // HD,
        ),
        name="attend",
    )(place, weights, queries, *kv_slots)


def finish_kernel(scale, last_ref, cotangent_ref, *refs):
    arrived_refs, handed_refs = refs[:PARTS], refs[PARTS : 2 * PARTS]
    out_ref, share_ref, cotangent, stream, arrived_last, sems = refs[2 * PARTS :]
    rows, features = stream.shape
    last_copy = pltpu.make_async_copy(arrived_refs[-1], arrived_last, sems.at[0])
    last_copy.start()
    cotangent_copy = pltpu.make_async_copy(cotangent_ref, cotangent, sems.at[1])
    cotangent_copy.start()
    is_last = last_ref[0] == 1
    squares = jnp.zeros((rows, HD), jnp.float32)
    done = 0
    for part in range(PARTS):
        source = arrived_refs[part]
        if part == PARTS - 1:
            last_copy.wait()
            source = arrived_last
        for column in range(0, source.shape[1], HD):
            handed = handed_refs[part][:, pl.ds(column, HD)].astype(jnp.float32)
            arrived = source[:, pl.ds(column, HD)].astype(jnp.float32)
            total = jnp.where(is_last, handed + arrived, handed).astype(jnp.bfloat16)
            stream[:, pl.ds(done + column, HD)] = total
            widened = total.astype(jnp.float32)
            squares += widened * widened
        done += source.shape[1]
    store_copy = pltpu.make_async_copy(stream, out_ref, sems.at[2])
    store_copy.start()
    mean = jnp.sum(squares, axis=1, keepdims=True) / features
    inverse = lax.rsqrt(mean + 1e-06) * scale
    cotangent_copy.wait()
    for tile in range(features // HD):
        columns = pl.ds(tile * HD, HD)
        term = cotangent[:, columns].astype(jnp.float32) * stream[:, columns].astype(jnp.float32)
        share_ref[pl.ds(tile, 1), :] = jnp.sum(term * inverse, axis=0, keepdims=True)
    store_copy.wait()


def finish(is_last, cotangent, arrived, handed, scale):
    rows, features = cotangent.shape
    return pl.pallas_call(
        functools.partial(finish_kernel, scale),
        out_shape=(
            jax.ShapeDtypeStruct((rows, features), jnp.bfloat16),
            jax.ShapeDtypeStruct((features // HD, HD), jnp.float32),
        ),
        in_specs=[SMEM, ANY] + [VMEM] * (PARTS - 1) + [ANY] + [VMEM] * PARTS,
        out_specs=(ANY, VMEM),
        scratch_shapes=[
            pltpu.VMEM((rows, features), jnp.bfloat16),
            pltpu.VMEM((rows, features), jnp.bfloat16),
            pltpu.VMEM(arrived[-1].shape, jnp.bfloat16),
            pltpu.SemaphoreType.DMA((3,)),
        ],
        compiler_params=pltpu.CompilerParams(vmem_limit_bytes=16 << 20),
        cost_estimate=pl.CostEstimate(
            flops=10 * rows * features, bytes_accessed=8 * rows * features, transcendentals=rows
        ),
        name="finish",
    )(is_last, cotangent, *arrived, *handed)


def swapped_sum(value, axis, distances):
    count = lax.axis_size(axis)
    for distance in distances:
        value = value + lax.ppermute(value, axis, [(place, place ^ distance) for place in range(count)])
    return value


def powers(first, end):
    return [1 << step for step in range(first, (end - 1).bit_length())]


def total_share(value):
    replicas, count = lax.axis_size("dp"), lax.axis_size("ctx")
    value = swapped_sum(value, "dp", [1])
    if replicas != 4 or count > 4:
        return swapped_sum(swapped_sum(value, "dp", powers(1, replicas)), "ctx", powers(0, count))
    core = lax.axis_index("dp") % 2
    heard = []
    for distance in range(count):
        pairs = []
        for replica in range(replicas):
            for place in range(count):
                across = replica ^ 2 if distance == 0 or replica % 2 else replica
                pairs.append((replica * count + place, across * count + (place ^ distance)))
        heard.append(lax.ppermute(value, ("dp", "ctx"), pairs))
    value = sum(heard[1:], jnp.where(core == 0, value + heard[0], 0.0))
    return swapped_sum(value, "dp", [1])


def fetch(value, slot):
    count, replicas = lax.axis_size("ctx"), lax.axis_size("dp")
    pairs = []
    for replica in range(replicas):
        for place in range(count):
            near = abs(place - (place ^ slot)) <= count // 2
            partner = (replica, place ^ slot) if near else (replica ^ 1, place)
            pairs.append((replica * count + place, partner[0] * count + partner[1]))
    return lax.ppermute(value, ("dp", "ctx"), pairs)


def gather_slots(value):
    return [value] + [fetch(value, slot) for slot in range(1, lax.axis_size("ctx"))]


def per_device(queries, keys_values, random_blocks, global_blocks, doc_lengths, cotangent):
    queries, keys_values, cotangent = queries[0, 0], keys_values[0, 0], cotangent[0, 0]
    place = lax.axis_index("ctx").astype(jnp.int32).reshape(1)
    scalars = (place, random_blocks, global_blocks, doc_lengths)
    section_count = lax.axis_size("section")
    section_place = lax.axis_index("section")
    half = KVH * HD
    early_width = EARLY * HD
    early_heads, late_heads = GROUPS
    weights = weigh(scalars, queries.shape[0], lax.axis_size("ctx"))
    first_hop = [(0, 1), (1, 0)]
    kv_parts = []
    for heads in GROUPS:
        first, last = heads[0] * HD, (heads[-1] + 1) * HD
        kv_parts.append(
            jnp.concatenate([keys_values[:, first:last], keys_values[:, half + first : half + last]], axis=1)
        )
    early_kv = lax.ppermute(kv_parts[0], "section", first_hop)
    part_queries = queries[:, : EARLY * GROUP * HD]
    early_queries = lax.ppermute(part_queries, "section", first_hop)
    late_slots = gather_slots(kv_parts[1])
    both = jnp.concatenate([kv_parts[0], early_kv], axis=1)
    late_slots[1], early_kv = lax.optimization_barrier((late_slots[1], early_kv))
    late_columns = EARLY * GROUP * HD
    late = attend(
        late_heads, place, weights, queries, late_columns, late_slots, 0, half - early_width, 120, True
    )
    arrived_late = lax.ppermute(late, "section", first_hop)
    if lax.axis_size("ctx") == 4:
        first, third = fetch(both, 1), lax.ppermute(both, "ctx", [(1, 2), (2, 1)])
        first, early_queries = lax.optimization_barrier((first, early_queries))
        both_slots = [both, first, fetch(first, 3), third, fetch(third, 1)]
    else:
        both_slots = gather_slots(both)
    own = attend(early_heads, place, weights, part_queries, 0, both_slots, 0, early_width, 1)
    early = attend(
        early_heads, place, weights, early_queries, 0, both_slots, 2 * early_width, 3 * early_width, 1
    )
    arrived = [early, arrived_late]
    handed = [own, late]
    for step in range(2, section_count):
        on_step = section_place == step - 1
        for part in range(PARTS):
            total = handed[part].astype(jnp.float32) + arrived[part].astype(jnp.float32)
            handed[part] = jnp.where(on_step, total.astype(jnp.bfloat16), handed[part])
            arrived[part] = lax.ppermute(handed[part], "section", [(step - 1, step), (step, step - 1)])
    is_last = (section_place == section_count - 1).astype(jnp.int32).reshape(1)
    stream, share = finish(is_last, cotangent, arrived, handed, 1.0 / lax.axis_size("dp"))
    gain_grad = total_share(share)
    return (stream[None, None], gain_grad.reshape(1, HEADS * HD))


def solution(mesh):
    in_specs = (
        P("section", "dp", "ctx", None),
        P("section", "dp", "ctx", None),
        P("dp", None, None, None),
        P("dp", None),
        P("dp", None),
        P("section", "dp", "ctx", None),
    )
    out_specs = (P("section", "dp", "ctx", None), P("section", None))
    return jax.shard_map(
        per_device, mesh=mesh, in_specs=in_specs, out_specs=out_specs, check_vma=False
    )
```

```python
import functools
import math

import jax
import jax.numpy as jnp
from jax import lax
from jax.experimental import pallas as pl
from jax.experimental.pallas import tpu as pltpu
from jax.sharding import PartitionSpec as P

HEADS = 32
KVH = 4
HD = 128
RAND = 4
GLOBALS = 2
GROUP = 8
EARLY = 2
GROUPS = (range(EARLY), range(EARLY, KVH))
PARTS = len(GROUPS)
NEVER = -1e30
LEVELS = 8
SCALE = math.log2(math.e) / math.sqrt(HD)
VMEM = pl.BlockSpec(memory_space=pltpu.VMEM)
SMEM = pl.BlockSpec(memory_space=pltpu.SMEM)
ANY = pl.BlockSpec(memory_space=pl.ANY)


def count_docs(doc_ends, positions):
    found = jnp.zeros(positions.shape, jnp.int32)
    for end in doc_ends:
        found += (positions >= end).astype(jnp.int32)
    return found


def weigh_kernel(place_ref, lists_ref, globals_ref, docs_ref, out_ref):
    rows, width = out_ref.shape[0] - LEVELS, out_ref.shape[1]
    place = place_ref[0]
    doc_ends, end = [], 0
    for doc in range(docs_ref.shape[1]):
        end = end + docs_ref[0, doc]
        doc_ends.append(end)
    query_doc = count_docs(doc_ends, place * rows + lax.broadcasted_iota(jnp.int32, (rows, 1), 0))
    for slot in range(width // rows):
        block = place ^ slot
        columns = pl.ds(slot * rows, rows)
        key_doc = count_docs(doc_ends, block * rows + lax.broadcasted_iota(jnp.int32, (1, rows), 1))
        out_ref[pl.ds(0, rows), columns] = jnp.where(query_doc == key_doc, 0.0, NEVER)
        shared = (jnp.abs(block - place) <= 1).astype(jnp.int32)
        for entry in range(GLOBALS):
            shared += (globals_ref[0, entry] == block).astype(jnp.int32)
        for head in range(KVH):
            times = shared
            for entry in range(RAND):
                times += (lists_ref[0, place, head, entry] == block).astype(jnp.int32)
            times = jnp.full((1, rows), times, jnp.int32)
            level = jnp.where(times > 0, jnp.log2(times.astype(jnp.float32)), NEVER)
            out_ref[pl.ds(rows + head, 1), columns] = level


def weigh(scalars, rows, slots):
    return pl.pallas_call(
        weigh_kernel,
        out_shape=jax.ShapeDtypeStruct((rows + LEVELS, slots * rows), jnp.float32),
        in_specs=[SMEM] * 4,
        out_specs=VMEM,
        compiler_params=pltpu.CompilerParams(vmem_limit_bytes=16 << 20),
        name="weigh",
    )(*scalars)


def attend_kernel(heads, query_base, key_base, value_base, kv_count, place_ref, weights_ref, q_ref, *refs):
    kv_refs, out_ref, scratch = refs[:kv_count], refs[kv_count], refs[kv_count + 1 :]
    rows = q_ref.shape[0]
    copies = []
    if scratch:
        for index in range(len(heads)):
            columns = pl.ds(index * GROUP * HD, GROUP * HD)
            source = q_ref.at[:, pl.ds(query_base + index * GROUP * HD, GROUP * HD)]
            copies.append(pltpu.make_async_copy(source, scratch[0].at[:, columns], scratch[1].at[index]))
            copies[-1].start()
        q_ref, query_base = scratch[0], 0
    slots = weights_ref.shape[1] // rows
    at_end = (place_ref[0] == 0) | (place_ref[0] == slots - 1)

    def blocks(column):
        found = [ref[:, pl.ds(column, HD)] for ref in kv_refs]
        if len(found) > slots:
            found[2] = jnp.where(at_end, found[slots], found[2])
        return jnp.concatenate(found[:slots], axis=0)

    for index, head in enumerate(heads):
        bias = weights_ref[pl.ds(0, rows), :] + weights_ref[pl.ds(rows + head, 1), :]
        bias = jnp.concatenate([bias, bias], axis=0)
        keys = blocks(key_base + index * HD)
        values = blocks(value_base + index * HD)
        values = jnp.concatenate([values, jnp.ones_like(values)], axis=1)
        if copies:
            copies[index].wait()
        for pair in range(GROUP // 2):
            first = (index * GROUP + 2 * pair) * HD
            source = query_base + first
            query = jnp.concatenate(
                [q_ref[:, pl.ds(source, HD)], q_ref[:, pl.ds(source + HD, HD)]], axis=0
            )
            scores = lax.dot_general(
                query, keys, (((1,), (1,)), ((), ())), preferred_element_type=jnp.float32
            )
            scores = scores * SCALE + bias
            weights = jnp.exp2(scores - jnp.max(scores, axis=1, keepdims=True))
            product = jnp.dot(
                weights.astype(jnp.bfloat16), values, preferred_element_type=jnp.float32
            )
            result = (product[:, :HD] / product[:, HD:]).astype(jnp.bfloat16)
            out_ref[:, pl.ds(first, HD)] = result[:rows]
            out_ref[:, pl.ds(first + HD, HD)] = result[rows:]


def attend(heads, place, weights, queries, query_base, kv_slots, key_base, value_base, effort, fetched=False):
    rows, width = queries.shape[0], len(heads) * GROUP * HD
    keys = weights.shape[1]
    return pl.pallas_call(
        functools.partial(attend_kernel, heads, query_base, key_base, value_base, len(kv_slots)),
        out_shape=jax.ShapeDtypeStruct((rows, width), jnp.bfloat16),
        in_specs=[SMEM, VMEM, ANY if fetched else VMEM] + [VMEM] * len(kv_slots),
        out_specs=VMEM,
        scratch_shapes=[
            pltpu.VMEM((rows, width), jnp.bfloat16),
            pltpu.SemaphoreType.DMA((len(heads),)),
        ]
        if fetched
        else [],
        compiler_params=pltpu.CompilerParams(vmem_limit_bytes=(16 if fetched else 16) << 20),
        cost_estimate=pl.CostEstimate(
            flops=effort * rows * width * keys,
            bytes_accessed=4 * rows * width + 4 * keys * len(heads) * HD,
            transcendentals=rows * width * keys // HD,
        ),
        name="attend",
    )(place, weights, queries, *kv_slots)


def finish_kernel(scale, last_ref, cotangent_ref, *refs):
    arrived_refs, handed_refs = refs[:PARTS], refs[PARTS : 2 * PARTS]
    out_ref, share_ref, cotangent, stream, arrived_last, sems = refs[2 * PARTS :]
    rows, features = stream.shape
    last_copy = pltpu.make_async_copy(arrived_refs[-1], arrived_last, sems.at[0])
    last_copy.start()
    cotangent_copy = pltpu.make_async_copy(cotangent_ref, cotangent, sems.at[1])
    cotangent_copy.start()
    is_last = last_ref[0] == 1
    squares = jnp.zeros((rows, HD), jnp.float32)
    done = 0
    for part in range(PARTS):
        source = arrived_refs[part]
        if part == PARTS - 1:
            last_copy.wait()
            source = arrived_last
        for column in range(0, source.shape[1], HD):
            handed = handed_refs[part][:, pl.ds(column, HD)].astype(jnp.float32)
            arrived = source[:, pl.ds(column, HD)].astype(jnp.float32)
            total = jnp.where(is_last, handed + arrived, handed).astype(jnp.bfloat16)
            stream[:, pl.ds(done + column, HD)] = total
            widened = total.astype(jnp.float32)
            squares += widened * widened
        done += source.shape[1]
    store_copy = pltpu.make_async_copy(stream, out_ref, sems.at[2])
    store_copy.start()
    mean = jnp.sum(squares, axis=1, keepdims=True) / features
    inverse = lax.rsqrt(mean + 1e-06) * scale
    cotangent_copy.wait()
    for tile in range(features // HD):
        columns = pl.ds(tile * HD, HD)
        term = cotangent[:, columns].astype(jnp.float32) * stream[:, columns].astype(jnp.float32)
        share_ref[pl.ds(tile, 1), :] = jnp.sum(term * inverse, axis=0, keepdims=True)
    store_copy.wait()


def finish(is_last, cotangent, arrived, handed, scale):
    rows, features = cotangent.shape
    return pl.pallas_call(
        functools.partial(finish_kernel, scale),
        out_shape=(
            jax.ShapeDtypeStruct((rows, features), jnp.bfloat16),
            jax.ShapeDtypeStruct((features // HD, HD), jnp.float32),
        ),
        in_specs=[SMEM, ANY] + [VMEM] * (PARTS - 1) + [ANY] + [VMEM] * PARTS,
        out_specs=(ANY, VMEM),
        scratch_shapes=[
            pltpu.VMEM((rows, features), jnp.bfloat16),
            pltpu.VMEM((rows, features), jnp.bfloat16),
            pltpu.VMEM(arrived[-1].shape, jnp.bfloat16),
            pltpu.SemaphoreType.DMA((3,)),
        ],
        compiler_params=pltpu.CompilerParams(vmem_limit_bytes=16 << 20),
        cost_estimate=pl.CostEstimate(
            flops=10 * rows * features, bytes_accessed=8 * rows * features, transcendentals=rows
        ),
        name="finish",
    )(is_last, cotangent, *arrived, *handed)


def swapped_sum(value, axis, distances):
    count = lax.axis_size(axis)
    for distance in distances:
        value = value + lax.ppermute(value, axis, [(place, place ^ distance) for place in range(count)])
    return value


def powers(first, end):
    return [1 << step for step in range(first, (end - 1).bit_length())]


def total_share(value):
    replicas, count = lax.axis_size("dp"), lax.axis_size("ctx")
    value = swapped_sum(value, "dp", [1])
    if replicas != 4 or count > 4:
        return swapped_sum(swapped_sum(value, "dp", powers(1, replicas)), "ctx", powers(0, count))
    core = lax.axis_index("dp") % 2
    heard = []
    for distance in range(count):
        pairs = []
        for replica in range(replicas):
            for place in range(count):
                across = replica ^ 2 if distance == 0 or replica % 2 else replica
                pairs.append((replica * count + place, across * count + (place ^ distance)))
        heard.append(lax.ppermute(value, ("dp", "ctx"), pairs))
    value = sum(heard[1:], jnp.where(core == 0, value + heard[0], 0.0))
    return swapped_sum(value, "dp", [1])


def fetch(value, slot):
    count, replicas = lax.axis_size("ctx"), lax.axis_size("dp")
    pairs = []
    for replica in range(replicas):
        for place in range(count):
            near = abs(place - (place ^ slot)) <= count // 2
            partner = (replica, place ^ slot) if near else (replica ^ 1, place)
            pairs.append((replica * count + place, partner[0] * count + partner[1]))
    return lax.ppermute(value, ("dp", "ctx"), pairs)


def gather_slots(value):
    slots = [fetch(value, slot) for slot in range(lax.axis_size("ctx") - 1, 0, -1)]
    return [value] + slots[::-1]


def per_device(queries, keys_values, random_blocks, global_blocks, doc_lengths, cotangent):
    queries, keys_values, cotangent = queries[0, 0], keys_values[0, 0], cotangent[0, 0]
    place = lax.axis_index("ctx").astype(jnp.int32).reshape(1)
    scalars = (place, random_blocks, global_blocks, doc_lengths)
    section_count = lax.axis_size("section")
    section_place = lax.axis_index("section")
    half = KVH * HD
    early_width = EARLY * HD
    early_heads, late_heads = GROUPS
    weights = weigh(scalars, queries.shape[0], lax.axis_size("ctx"))
    first_hop = [(0, 1), (1, 0)]
    kv_parts = []
    for heads in GROUPS:
        first, last = heads[0] * HD, (heads[-1] + 1) * HD
        kv_parts.append(
            jnp.concatenate([keys_values[:, first:last], keys_values[:, half + first : half + last]], axis=1)
        )
    early_kv = lax.ppermute(kv_parts[0], "section", first_hop)
    part_queries = queries[:, : EARLY * GROUP * HD]
    early_queries = lax.ppermute(part_queries, "section", first_hop)
    late_slots = gather_slots(kv_parts[1])
    both = jnp.concatenate([kv_parts[0], early_kv], axis=1)
    late_slots[-1], early_kv = lax.optimization_barrier((late_slots[-1], early_kv))
    late_columns = EARLY * GROUP * HD
    late = attend(
        late_heads, place, weights, queries, late_columns, late_slots, 0, half - early_width, 120, True
    )
    arrived_late = lax.ppermute(late, "section", first_hop)
    if lax.axis_size("ctx") == 4:
        first, third = fetch(both, 1), lax.ppermute(both, "ctx", [(1, 2), (2, 1)])
        first, early_queries = lax.optimization_barrier((first, early_queries))
        both_slots = [both, first, fetch(first, 3), third, fetch(third, 1)]
    else:
        both_slots = gather_slots(both)
    own = attend(early_heads, place, weights, part_queries, 0, both_slots, 0, early_width, 1)
    early = attend(
        early_heads, place, weights, early_queries, 0, both_slots, 2 * early_width, 3 * early_width, 1
    )
    arrived = [early, arrived_late]
    handed = [own, late]
    for step in range(2, section_count):
        on_step = section_place == step - 1
        for part in range(PARTS):
            total = handed[part].astype(jnp.float32) + arrived[part].astype(jnp.float32)
            handed[part] = jnp.where(on_step, total.astype(jnp.bfloat16), handed[part])
            arrived[part] = lax.ppermute(handed[part], "section", [(step - 1, step), (step, step - 1)])
    is_last = (section_place == section_count - 1).astype(jnp.int32).reshape(1)
    stream, share = finish(is_last, cotangent, arrived, handed, 1.0 / lax.axis_size("dp"))
    gain_grad = total_share(share)
    return (stream[None, None], gain_grad.reshape(1, HEADS * HD))


def solution(mesh):
    in_specs = (
        P("section", "dp", "ctx", None),
        P("section", "dp", "ctx", None),
        P("dp", None, None, None),
        P("dp", None),
        P("dp", None),
        P("section", "dp", "ctx", None),
    )
    out_specs = (P("section", "dp", "ctx", None), P("section", None))
    return jax.shard_map(
        per_device, mesh=mesh, in_specs=in_specs, out_specs=out_specs, check_vma=False
    )
```

```python
import functools
import math

import jax
import jax.numpy as jnp
from jax import lax
from jax.experimental import pallas as pl
from jax.experimental.pallas import tpu as pltpu
from jax.sharding import PartitionSpec as P

HEADS = 32
KVH = 4
HD = 128
RAND = 4
GLOBALS = 2
GROUP = 8
EARLY = 2
GROUPS = (range(EARLY), range(EARLY, KVH))
PARTS = len(GROUPS)
LAST_COPIES = 2
NEVER = -1e30
LEVELS = 8
SCALE = math.log2(math.e) / math.sqrt(HD)
VMEM = pl.BlockSpec(memory_space=pltpu.VMEM)
SMEM = pl.BlockSpec(memory_space=pltpu.SMEM)
ANY = pl.BlockSpec(memory_space=pl.ANY)


def count_docs(doc_ends, positions):
    found = jnp.zeros(positions.shape, jnp.int32)
    for end in doc_ends:
        found += (positions >= end).astype(jnp.int32)
    return found


def weigh_kernel(place_ref, lists_ref, globals_ref, docs_ref, out_ref):
    rows, width = out_ref.shape[0] - LEVELS, out_ref.shape[1]
    place = place_ref[0]
    doc_ends, end = [], 0
    for doc in range(docs_ref.shape[1]):
        end = end + docs_ref[0, doc]
        doc_ends.append(end)
    query_doc = count_docs(doc_ends, place * rows + lax.broadcasted_iota(jnp.int32, (rows, 1), 0))
    for slot in range(width // rows):
        block = place ^ slot
        columns = pl.ds(slot * rows, rows)
        key_doc = count_docs(doc_ends, block * rows + lax.broadcasted_iota(jnp.int32, (1, rows), 1))
        out_ref[pl.ds(0, rows), columns] = jnp.where(query_doc == key_doc, 0.0, NEVER)
        shared = (jnp.abs(block - place) <= 1).astype(jnp.int32)
        for entry in range(GLOBALS):
            shared += (globals_ref[0, entry] == block).astype(jnp.int32)
        for head in range(KVH):
            times = shared
            for entry in range(RAND):
                times += (lists_ref[0, place, head, entry] == block).astype(jnp.int32)
            times = jnp.full((1, rows), times, jnp.int32)
            level = jnp.where(times > 0, jnp.log2(times.astype(jnp.float32)), NEVER)
            out_ref[pl.ds(rows + head, 1), columns] = level


def weigh(scalars, rows, slots):
    return pl.pallas_call(
        weigh_kernel,
        out_shape=jax.ShapeDtypeStruct((rows + LEVELS, slots * rows), jnp.float32),
        in_specs=[SMEM] * 4,
        out_specs=VMEM,
        compiler_params=pltpu.CompilerParams(vmem_limit_bytes=16 << 20),
        name="weigh",
    )(*scalars)


def attend_kernel(heads, query_base, key_base, value_base, kv_count, place_ref, weights_ref, q_ref, *refs):
    kv_refs, out_ref, scratch = refs[:kv_count], refs[kv_count], refs[kv_count + 1 :]
    rows = q_ref.shape[0]
    copies = []
    if scratch:
        for index in range(len(heads)):
            columns = pl.ds(index * GROUP * HD, GROUP * HD)
            source = q_ref.at[:, pl.ds(query_base + index * GROUP * HD, GROUP * HD)]
            copies.append(pltpu.make_async_copy(source, scratch[0].at[:, columns], scratch[1].at[index]))
            copies[-1].start()
        q_ref, query_base = scratch[0], 0
    slots = weights_ref.shape[1] // rows
    at_end = (place_ref[0] == 0) | (place_ref[0] == slots - 1)

    def blocks(column):
        found = [ref[:, pl.ds(column, HD)] for ref in kv_refs]
        if len(found) > slots:
            found[2] = jnp.where(at_end, found[slots], found[2])
        return jnp.concatenate(found[:slots], axis=0)

    for index, head in enumerate(heads):
        bias = weights_ref[pl.ds(0, rows), :] + weights_ref[pl.ds(rows + head, 1), :]
        bias = jnp.concatenate([bias, bias], axis=0)
        keys = blocks(key_base + index * HD)
        values = blocks(value_base + index * HD)
        values = jnp.concatenate([values, jnp.ones_like(values)], axis=1)
        if copies:
            copies[index].wait()
        for pair in range(GROUP // 2):
            first = (index * GROUP + 2 * pair) * HD
            source = query_base + first
            query = jnp.concatenate(
                [q_ref[:, pl.ds(source, HD)], q_ref[:, pl.ds(source + HD, HD)]], axis=0
            )
            scores = lax.dot_general(
                query, keys, (((1,), (1,)), ((), ())), preferred_element_type=jnp.float32
            )
            scores = scores * SCALE + bias
            weights = jnp.exp2(scores - jnp.max(scores, axis=1, keepdims=True))
            product = jnp.dot(
                weights.astype(jnp.bfloat16), values, preferred_element_type=jnp.float32
            )
            result = (product[:, :HD] / product[:, HD:]).astype(jnp.bfloat16)
            out_ref[:, pl.ds(first, HD)] = result[:rows]
            out_ref[:, pl.ds(first + HD, HD)] = result[rows:]


def attend(heads, place, weights, queries, query_base, kv_slots, key_base, value_base, effort, fetched=False):
    rows, width = queries.shape[0], len(heads) * GROUP * HD
    keys = weights.shape[1]
    return pl.pallas_call(
        functools.partial(attend_kernel, heads, query_base, key_base, value_base, len(kv_slots)),
        out_shape=jax.ShapeDtypeStruct((rows, width), jnp.bfloat16),
        in_specs=[SMEM, VMEM, ANY if fetched else VMEM] + [VMEM] * len(kv_slots),
        out_specs=VMEM,
        scratch_shapes=[
            pltpu.VMEM((rows, width), jnp.bfloat16),
            pltpu.SemaphoreType.DMA((len(heads),)),
        ]
        if fetched
        else [],
        compiler_params=pltpu.CompilerParams(vmem_limit_bytes=(16 if fetched else 16) << 20),
        cost_estimate=pl.CostEstimate(
            flops=effort * rows * width * keys,
            bytes_accessed=4 * rows * width + 4 * keys * len(heads) * HD,
            transcendentals=rows * width * keys // HD,
        ),
        name="attend",
    )(place, weights, queries, *kv_slots)


def finish_kernel(scale, last_ref, cotangent_ref, *refs):
    arrived_refs, handed_refs = refs[:PARTS], refs[PARTS : 2 * PARTS]
    out_ref, share_ref, stream, arrived_last, sems = refs[2 * PARTS :]
    rows, features = stream.shape
    last_copies = []
    for index in range(LAST_COPIES):
        columns = pl.ds(index * (arrived_last.shape[1] // LAST_COPIES), arrived_last.shape[1] // LAST_COPIES)
        source = arrived_refs[-1].at[:, columns]
        last_copies.append(pltpu.make_async_copy(source, arrived_last.at[:, columns], sems.at[2 + index]))
        last_copies[-1].start()
    is_last = last_ref[0] == 1
    squares = jnp.zeros((rows, HD), jnp.float32)
    done = 0
    for part in range(PARTS):
        source = arrived_refs[part]
        if part == PARTS - 1:
            source = arrived_last
        for column in range(0, source.shape[1], HD):
            if part == PARTS - 1 and column % (source.shape[1] // LAST_COPIES) == 0:
                last_copies[column // (source.shape[1] // LAST_COPIES)].wait()
            handed = handed_refs[part][:, pl.ds(column, HD)].astype(jnp.float32)
            arrived = source[:, pl.ds(column, HD)].astype(jnp.float32)
            total = jnp.where(is_last, handed + arrived, handed).astype(jnp.bfloat16)
            stream[:, pl.ds(done + column, HD)] = total
            widened = total.astype(jnp.float32)
            squares += widened * widened
        done += source.shape[1]
    store_copy = pltpu.make_async_copy(stream, out_ref, sems.at[0])
    store_copy.start()
    mean = jnp.sum(squares, axis=1, keepdims=True) / features
    inverse = lax.rsqrt(mean + 1e-06) * scale
    for tile in range(features // HD):
        columns = pl.ds(tile * HD, HD)
        term = cotangent_ref[:, columns].astype(jnp.float32) * stream[:, columns].astype(jnp.float32)
        share_ref[pl.ds(tile, 1), :] = jnp.sum(term * inverse, axis=0, keepdims=True)
    store_copy.wait()


def finish(is_last, cotangent, arrived, handed, scale):
    rows, features = cotangent.shape
    return pl.pallas_call(
        functools.partial(finish_kernel, scale),
        out_shape=(
            jax.ShapeDtypeStruct((rows, features), jnp.bfloat16),
            jax.ShapeDtypeStruct((features // HD, HD), jnp.float32),
        ),
        in_specs=[SMEM, VMEM] + [VMEM] * (PARTS - 1) + [ANY] + [VMEM] * PARTS,
        out_specs=(ANY, VMEM),
        scratch_shapes=[
            pltpu.VMEM((rows, features), jnp.bfloat16),
            pltpu.VMEM(arrived[-1].shape, jnp.bfloat16),
            pltpu.SemaphoreType.DMA((2 + LAST_COPIES,)),
        ],
        compiler_params=pltpu.CompilerParams(vmem_limit_bytes=16 << 20),
        cost_estimate=pl.CostEstimate(
            flops=10 * rows * features, bytes_accessed=8 * rows * features, transcendentals=rows
        ),
        name="finish",
    )(is_last, cotangent, *arrived, *handed)


def swapped_sum(value, axis, distances):
    count = lax.axis_size(axis)
    for distance in distances:
        value = value + lax.ppermute(value, axis, [(place, place ^ distance) for place in range(count)])
    return value


def powers(first, end):
    return [1 << step for step in range(first, (end - 1).bit_length())]


def total_share(value):
    replicas, count = lax.axis_size("dp"), lax.axis_size("ctx")
    value = swapped_sum(value, "dp", [1])
    if replicas != 4 or count > 4:
        return swapped_sum(swapped_sum(value, "dp", powers(1, replicas)), "ctx", powers(0, count))
    core = lax.axis_index("dp") % 2
    heard = []
    for distance in range(count):
        pairs = []
        for replica in range(replicas):
            for place in range(count):
                across = replica ^ 2 if distance == 0 or replica % 2 else replica
                pairs.append((replica * count + place, across * count + (place ^ distance)))
        heard.append(lax.ppermute(value, ("dp", "ctx"), pairs))
    value = sum(heard[1:], jnp.where(core == 0, value + heard[0], 0.0))
    return swapped_sum(value, "dp", [1])


def fetch(value, slot):
    count, replicas = lax.axis_size("ctx"), lax.axis_size("dp")
    pairs = []
    for replica in range(replicas):
        for place in range(count):
            near = abs(place - (place ^ slot)) <= count // 2
            partner = (replica, place ^ slot) if near else (replica ^ 1, place)
            pairs.append((replica * count + place, partner[0] * count + partner[1]))
    return lax.ppermute(value, ("dp", "ctx"), pairs)


def gather_slots(value):
    slots = [fetch(value, slot) for slot in range(lax.axis_size("ctx") - 1, 0, -1)]
    return [value] + slots[::-1]


def per_device(queries, keys_values, random_blocks, global_blocks, doc_lengths, cotangent):
    queries, keys_values, cotangent = queries[0, 0], keys_values[0, 0], cotangent[0, 0]
    place = lax.axis_index("ctx").astype(jnp.int32).reshape(1)
    scalars = (place, random_blocks, global_blocks, doc_lengths)
    section_count = lax.axis_size("section")
    section_place = lax.axis_index("section")
    half = KVH * HD
    early_width = EARLY * HD
    early_heads, late_heads = GROUPS
    weights = weigh(scalars, queries.shape[0], lax.axis_size("ctx"))
    first_hop = [(0, 1), (1, 0)]
    kv_parts = []
    for heads in GROUPS:
        first, last = heads[0] * HD, (heads[-1] + 1) * HD
        kv_parts.append(
            jnp.concatenate([keys_values[:, first:last], keys_values[:, half + first : half + last]], axis=1)
        )
    early_kv = lax.ppermute(kv_parts[0], "section", first_hop)
    part_queries = queries[:, : EARLY * GROUP * HD]
    early_queries = lax.ppermute(part_queries, "section", first_hop)
    late_slots = gather_slots(kv_parts[1])
    both = jnp.concatenate([kv_parts[0], early_kv], axis=1)
    late_slots[-1], early_kv = lax.optimization_barrier((late_slots[-1], early_kv))
    late_columns = EARLY * GROUP * HD
    late = attend(
        late_heads, place, weights, queries, late_columns, late_slots, 0, half - early_width, 120, True
    )
    arrived_late = lax.ppermute(late, "section", first_hop)
    if lax.axis_size("ctx") == 4:
        first, third = fetch(both, 1), lax.ppermute(both, "ctx", [(1, 2), (2, 1)])
        first, early_queries = lax.optimization_barrier((first, early_queries))
        both_slots = [both, first, fetch(first, 3), third, fetch(third, 1)]
    else:
        both_slots = gather_slots(both)
    own = attend(early_heads, place, weights, part_queries, 0, both_slots, 0, early_width, 1)
    early = attend(
        early_heads, place, weights, early_queries, 0, both_slots, 2 * early_width, 3 * early_width, 1
    )
    arrived = [early, arrived_late]
    handed = [own, late]
    for step in range(2, section_count):
        on_step = section_place == step - 1
        for part in range(PARTS):
            total = handed[part].astype(jnp.float32) + arrived[part].astype(jnp.float32)
            handed[part] = jnp.where(on_step, total.astype(jnp.bfloat16), handed[part])
            arrived[part] = lax.ppermute(handed[part], "section", [(step - 1, step), (step, step - 1)])
    is_last = (section_place == section_count - 1).astype(jnp.int32).reshape(1)
    stream, share = finish(is_last, cotangent, arrived, handed, 1.0 / lax.axis_size("dp"))
    gain_grad = total_share(share)
    return (stream[None, None], gain_grad.reshape(1, HEADS * HD))


def solution(mesh):
    in_specs = (
        P("section", "dp", "ctx", None),
        P("section", "dp", "ctx", None),
        P("dp", None, None, None),
        P("dp", None),
        P("dp", None),
        P("section", "dp", "ctx", None),
    )
    out_specs = (P("section", "dp", "ctx", None), P("section", None))
    return jax.shard_map(
        per_device, mesh=mesh, in_specs=in_specs, out_specs=out_specs, check_vma=False
    )
```
